32 devices in a mesh: wave: 8 (over z, y), lev: 4 (over x, core).
Axes of the slice: x: 2, y: 2, z: 4, core: 2. Of those that a mesh axis runs over, the one named last changes fastest.
Arguments:
- fourier: float32 [2560, 6, 1088], P('wave', None, 'lev'), may hold values from -6 to 6
- weights: float32 [2560], P('wave'), may hold values from 0.3 to 3
- row_points: int32 [2560], replicated, may hold values from 20 to 5164, as said below
- slot_map: int32 [6], replicated, may hold values from 0 to 7, as said below
- legendre_lookup: float32 [8, 2, 640, 1280], P('wave'), may hold values from -0.15625 to 0.15625
- to_modes: float32 [136, 136], replicated, may hold values from -0.5 to 0.5
- from_modes: float32 [136, 136], replicated, may hold values from -0.5 to 0.5
- mode_rates: float32 [136], replicated, may hold values from 0.1 to 10
- thermal_response_matrix: float32 [136, 136], replicated, may hold values from -0.5 to 0.5
Outputs:
- spectra: float32 [8, 2, 640, 1088], P('wave', None, 'lev')
The draws below stay inside these ranges and needn't reach their ends.
Inputs may be any that keep to these rules, and one draw needn't show every extreme that they name: `row_points`: row t has 20 + 4 * d + 4 * q points, d its distance in rows from the nearer pole and q a whole number from 0 to 7; row 1279, the last row of the northern hemisphere, reaches the largest value. `slot_map`: distinct global slots; slot s is held by device s of wave (one slot per device); which slots, and so which devices, hold a wavenumber is drawn from the seed.
All inputs are finite; a program needn't handle non-finite values.
Results may differ from the reference program's by a relative error of at most 0.0003.
Values sent between devices are 32-bit elements; how exact they have to be, the bound alone decides.
A program may use at most 64 MiB of HBM per device.

```python
import math
import jax
import jax.numpy as jnp
from jax import lax

NTRUNC = 1280
LEVELS = 136
FIELDS = 4
LAT = 2560
LAT_H = 1280
NH = 640
M_WIN = 6
SLOTS_ALL = 8
COLS = 1088


def draw_row_points(key, part):
    hemisphere = LAT // 2
    places = jnp.arange(LAT, dtype=jnp.int32)
    polar_distance_rows = jnp.minimum(places, LAT - 1 - places)
    jitter = jax.random.randint(key, (LAT,), 0, 8).astype(jnp.int32)
    jitter = jitter.at[0].set(0).at[hemisphere - 1].set(7)
    return (20 + 4 * polar_distance_rows + 4 * jitter).astype(jnp.int32)


def draw_slot_map(key, part):
    first_key = jax.random.fold_in(key, 11)
    second_key = jax.random.fold_in(key, 12)
    inner = (jax.random.permutation(first_key, SLOTS_ALL - 2) + 1).astype(jnp.int32)
    chosen = jnp.concatenate([jnp.array([0, SLOTS_ALL - 1], dtype=jnp.int32), inner[:M_WIN - 2]])
    return chosen[jax.random.permutation(second_key, M_WIN)].astype(jnp.int32)


def block_levels(key, shape, pieces, low, top_value):
    gain, own = 1.0, jax.random.fold_in(key, 6)
    for dim, shards_of in pieces:
        draws = jnp.exp(jax.random.uniform(jax.random.fold_in(own, dim), (shards_of,), jnp.float32, low / len(pieces), top_value / len(pieces)))
        gain = gain * jnp.repeat(draws, shape[dim] // shards_of).reshape([-1 if axis == dim else 1 for axis in range(len(shape))])
    return gain


def normal_values(own_key, extent, deviation, most, shards=(), held_as=jnp.bfloat16):
    factor_of = block_levels(own_key, extent, shards, -0.22, 0.18) if shards else 1.0
    result = jax.random.normal(own_key, extent, jnp.float32) * deviation * factor_of
    return jnp.minimum(jnp.maximum(result, -most), most).astype(held_as)


def setup_inputs(seed: int = 0) -> dict:
    keys = jax.random.split(jax.random.key(seed), 10)
    fourier = normal_values(keys[0], (LAT, M_WIN, COLS), 1.0, 6.0, ((0, 8), (2, 4)), jnp.float32)
    weights = jnp.clip(jnp.exp(math.log(3.0) - 2.3025851 * jax.random.uniform(keys[1], (LAT,), jnp.float32) ** block_levels(keys[1], (LAT,), ((0, 8),), -0.2, 0.2)), 0.3, 3.0)
    row_points = draw_row_points(jax.random.fold_in(keys[9], 71), 0)
    slot_map = draw_slot_map(jax.random.fold_in(keys[9], 71), 0)
    legendre_lookup = normal_values(keys[4], (SLOTS_ALL, 2, NH, LAT_H), LAT_H ** -0.5, 0.15625, ((0, 8),), jnp.float32)
    to_modes = normal_values(keys[5], (LEVELS, LEVELS), LEVELS ** -0.5, 0.5, (), jnp.float32)
    from_modes = normal_values(keys[6], (LEVELS, LEVELS), LEVELS ** -0.5, 0.5, (), jnp.float32)
    mode_rates = jnp.clip(jnp.exp(jax.random.uniform(keys[7], (LEVELS,), jnp.float32, math.log(0.1), math.log(10.0))), 0.1, 10.0)
    thermal_response_matrix = normal_values(keys[8], (LEVELS, LEVELS), LEVELS ** -0.5, 0.5, (), jnp.float32)
    return dict(fourier=fourier, weights=weights, row_points=row_points, slot_map=slot_map, legendre_lookup=legendre_lookup, to_modes=to_modes, from_modes=from_modes, mode_rates=mode_rates, thermal_response_matrix=thermal_response_matrix)


def vertical_step(spectra, degree, to_modes, from_modes, mode_rates, thermal_response_matrix):
    maximal_wave_truncation = lax.Precision.HIGHEST
    layerwise_coefficients = spectra.reshape(spectra.shape[:-1] + (LEVELS, FIELDS, 2))
    divergence = layerwise_coefficients[..., 1, :]
    modal = jnp.einsum('kl,...lc->...kc', to_modes, divergence, precision=maximal_wave_truncation)
    degrees = degree.astype(jnp.float32)
    wave_ratio = degrees * (degrees + 1.0) / (NTRUNC * NTRUNC)
    damping = 1.0 / (1.0 + mode_rates * wave_ratio[..., None])
    advanced_flow_spreading = jnp.einsum('mc,...cb->...mb', from_modes, modal * damping[..., None], precision=maximal_wave_truncation)
    advanced_thermal_field = layerwise_coefficients[..., 2, :] - jnp.einsum('mc,...cb->...mb', thermal_response_matrix, advanced_flow_spreading, precision=maximal_wave_truncation)
    joined_coefficient_sets = jnp.stack([layerwise_coefficients[..., 0, :], advanced_flow_spreading, advanced_thermal_field, layerwise_coefficients[..., 3, :]], axis=-2)
    return joined_coefficient_sets.reshape(spectra.shape)


def reference(fourier, weights, row_points, slot_map, legendre_lookup, to_modes, from_modes, mode_rates, thermal_response_matrix):
    maximal_wave_truncation = lax.Precision.HIGHEST
    stride = NTRUNC // M_WIN
    wavenum = jnp.arange(M_WIN, dtype=jnp.int32) * stride
    retained = (2 * wavenum[None, :] < row_points[:, None]).astype(jnp.float32)
    scaling = weights[:, None] * retained
    slot_ids = jnp.arange(SLOTS_ALL, dtype=jnp.int32)
    matches = (slot_map[None, :] == slot_ids[:, None]).astype(jnp.int32)
    filled = jnp.sum(matches, axis=1)
    order = jnp.sum(matches * jnp.arange(M_WIN, dtype=jnp.int32)[None, :], axis=1)
    degree_base = order * stride
    row_ids = jnp.arange(NH, dtype=jnp.int32)
    parities = jnp.arange(2, dtype=jnp.int32)

    def one_member(packed):
        member_table, zonal_order_index, base_degree, filled_flag = packed
        factor = jnp.take(scaling, zonal_order_index, axis=1) * filled_flag.astype(jnp.float32)
        column = jnp.take(fourier, zonal_order_index, axis=1) * factor[:, None]
        northern = column[:LAT_H]
        southern = column[LAT_H:][::-1]
        paired = jnp.stack([northern + southern, northern - southern])
        sums = jnp.einsum('pih,phc->pic', member_table, paired, precision=maximal_wave_truncation)
        degree = base_degree + 2 * row_ids[None, :] + parities[:, None]
        validity = (degree < NTRUNC).astype(jnp.float32)
        sums = sums * validity[:, :, None]
        return vertical_step(sums, degree, to_modes, from_modes, mode_rates, thermal_response_matrix)

    return lax.map(one_member, (legendre_lookup, order, degree_base, filled))
```

```python
import functools
import jax
import jax.numpy as jnp
from jax import lax
from jax.experimental import pallas as pl
from jax.experimental.pallas import tpu as pltpu
from jax.sharding import PartitionSpec as P

NTRUNC = 1280
LEVELS = 136
FIELDS = 4


def vertical_step(spectra, degree, to_modes, from_modes, mode_rates, thermal_response_matrix):
    maximal_wave_truncation = lax.Precision.HIGHEST
    layerwise_coefficients = spectra.reshape(spectra.shape[:-1] + (LEVELS, FIELDS, 2))
    divergence = layerwise_coefficients[..., 1, :]
    modal = jnp.einsum("kl,...lc->...kc", to_modes, divergence, precision=maximal_wave_truncation)
    degrees = degree.astype(jnp.float32)
    wave_ratio = degrees * (degrees + 1.0) / (NTRUNC * NTRUNC)
    damping = 1.0 / (1.0 + mode_rates * wave_ratio[..., None])
    advanced_flow_spreading = jnp.einsum(
        "mc,...cb->...mb", from_modes, modal * damping[..., None], precision=maximal_wave_truncation
    )
    advanced_thermal_field = layerwise_coefficients[..., 2, :] - jnp.einsum(
        "mc,...cb->...mb",
        thermal_response_matrix,
        advanced_flow_spreading,
        precision=maximal_wave_truncation,
    )
    joined_coefficient_sets = jnp.stack(
        [
            layerwise_coefficients[..., 0, :],
            advanced_flow_spreading,
            advanced_thermal_field,
            layerwise_coefficients[..., 3, :],
        ],
        axis=-2,
    )
    return joined_coefficient_sets.reshape(spectra.shape)


def legendre_sums(paired, tables):
    maximal_wave_truncation = lax.Precision.HIGHEST
    return jnp.einsum("spih,phsc->spic", tables, paired, precision=maximal_wave_truncation)


def on_device_plain(
    fourier,
    weights,
    row_points,
    slot_map,
    legendre_lookup,
    to_modes,
    from_modes,
    mode_rates,
    thermal_response_matrix,
):
    wave_count = lax.axis_size("wave")
    layer_number = lax.axis_size("lev")
    wave_index = lax.axis_index("wave")
    level_index = lax.axis_index("lev")
    lat_local = fourier.shape[0]
    window = fourier.shape[1]
    columns = fourier.shape[2]
    slot_count = legendre_lookup.shape[0]
    half_rows = legendre_lookup.shape[2]
    lat_half = legendre_lookup.shape[3]
    all_slots = slot_count * wave_count
    lat_total = 2 * lat_half
    stride = NTRUNC // window
    wavenum = jnp.arange(window, dtype=jnp.int32) * stride
    points_here = lax.dynamic_slice_in_dim(row_points, wave_index * lat_local, lat_local, 0)
    retained = (2 * wavenum[None, :] < points_here[:, None]).astype(jnp.float32)
    weighted = fourier * (weights[:, None] * retained)[:, :, None]
    slot_ids = jnp.arange(all_slots, dtype=jnp.int32)
    matches = (slot_map[None, :] == slot_ids[:, None]).astype(jnp.int32)
    used_all = jnp.sum(matches, axis=1)
    source_all = jnp.sum(matches * jnp.arange(window, dtype=jnp.int32)[None, :], axis=1)
    outgoing = jnp.take(weighted, source_all, axis=1) * used_all.astype(jnp.float32)[None, :, None]
    outgoing = outgoing.reshape(lat_local, wave_count, slot_count, columns)
    arrived = lax.all_to_all(outgoing, "wave", split_axis=1, concat_axis=0, tiled=True)
    arrived = arrived.reshape(lat_total, slot_count, columns)
    northern = arrived[:lat_half]
    southern = arrived[lat_half:][::-1]
    paired = jnp.stack([northern + southern, northern - southern])
    owned_orders = lax.dynamic_slice_in_dim(source_all, wave_index * slot_count, slot_count, 0)
    degree_base = owned_orders * stride
    row_count = half_rows // layer_number
    row_start = level_index * row_count
    local_spectra = legendre_sums(paired, legendre_lookup)
    spectra = lax.all_to_all(local_spectra, "lev", split_axis=2, concat_axis=3, tiled=True)
    row_ids = row_start + jnp.arange(row_count, dtype=jnp.int32)
    parities = jnp.arange(2, dtype=jnp.int32)
    degree = degree_base[:, None, None] + 2 * row_ids[None, None, :] + parities[None, :, None]
    validity = (degree < NTRUNC).astype(jnp.float32)
    joined_coefficient_sets = vertical_step(
        spectra, degree, to_modes, from_modes, mode_rates, thermal_response_matrix
    )
    return joined_coefficient_sets * validity[..., None]


F32 = jnp.float32
BF16 = jnp.bfloat16
HALF_TILE = 64
LANES = 128
LAST = 128
MESH_IDS = pl.DeviceIdType.MESH


def split(x):
    high = x.astype(BF16)
    return high, (x - high.astype(F32)).astype(BF16)


def dot_nn(a, b):
    return lax.dot_general(a, b, (((1,), (0,)), ((), ())), preferred_element_type=F32)


def dot_nt(a, b):
    return lax.dot_general(a, b, (((1,), (1,)), ((), ())), preferred_element_type=F32)


def iota(shape, dim):
    return lax.broadcasted_iota(jnp.int32, shape, dim)


def one_hot(cond):
    return cond.astype(F32).astype(BF16)


def kernel(
    sizes,
    slot_map,
    weights,
    points,
    fourier,
    table_hbm,
    to_modes,
    from_modes,
    rates,
    thermal,
    out,
    table,
    table_hi,
    table_lo,
    outgoing,
    arrived,
    pair_hi,
    pair_lo,
    spec_a,
    spec_b,
    got_a,
    got_b,
    m_hi,
    m_lo,
    g_hi,
    g_lo,
    damp,
    modal,
    table_sem,
    wave_send,
    wave_recv,
    lev_send,
    lev_recv,
):
    wave_count, lev_count, chunks, wave_steps, lev_steps = sizes
    window, cols, lats = fourier.shape
    _, half_rows, lat_half = table_hbm.shape
    levels = to_modes.shape[0]
    all_cols = cols * lev_count
    mode_cols = 2 * levels
    rows = half_rows // lev_count
    stride = NTRUNC // window
    tiles = lats // LANES
    half_waves = wave_count // 2
    w = lax.axis_index("wave")
    v = lax.axis_index("lev")

    barrier = pltpu.get_barrier_semaphore()
    for k in wave_steps:
        pl.semaphore_signal(
            barrier, inc=1, device_id={"wave": lax.rem(w + k, wave_count)}, device_id_type=MESH_IDS
        )
    for k in lev_steps:
        pl.semaphore_signal(
            barrier, inc=1, device_id={"lev": lax.rem(v + k, lev_count)}, device_id_type=MESH_IDS
        )
    table_copy = pltpu.make_async_copy(table_hbm, table, table_sem)
    table_copy.start()

    def slot_source(slot):
        source = jnp.int32(0)
        used = jnp.int32(0)
        for j in range(window):
            hit = slot_map[j] == slot
            source = jnp.where(hit, j, source)
            used = jnp.where(hit, 1, used)
        return source, used

    south = (w >= half_waves).astype(jnp.int32)
    mirrored = w + south * (wave_count - 1 - 2 * w)
    odd = lax.rem(mirrored, 2)
    place = iota((lats, lats), 1) + odd * HALF_TILE
    place = jnp.where(place >= lats, place - lats, place)
    place = place + south * (lats - 1 - 2 * place)
    arrange = one_hot(iota((lats, lats), 0) == place)
    point_row = points[pl.ds(w, 1), :]
    weight_row = weights[...]

    def arranged(slot, first, width, write):
        source, used = slot_source(slot)
        keep = (2 * stride * source < point_row).astype(F32) * used.astype(F32)
        block = fourier[source, first : first + width, :] * (weight_row * keep)
        high, low = split(block)
        moved = dot_nn(high, arrange) + dot_nn(low, arrange)
        for t in range(tiles):
            write(t * width, width, moved[:, t * LANES : (t + 1) * LANES])
        left = moved[: width // 2, tiles * LANES :]
        right = moved[width // 2 :, tiles * LANES :]
        write(tiles * width, width // 2, jnp.concatenate([left, right], axis=1))

    def wave_copy(c, k):
        first, width, base, length = chunks[c]
        return pltpu.make_async_remote_copy(
            src_ref=outgoing.at[k - 1, pl.ds(base, length)],
            dst_ref=arrived.at[w, pl.ds(base, length)],
            send_sem=wave_send.at[c, k - 1],
            recv_sem=wave_recv.at[c, k - 1],
            device_id={"wave": lax.rem(w + k, wave_count)},
            device_id_type=MESH_IDS,
        )

    pl.semaphore_wait(barrier, len(wave_steps) + len(lev_steps))
    for c, (first, width, base, length) in enumerate(chunks):
        for k in wave_steps:

            def put(at, count, value, k=k, base=base):
                outgoing[k - 1, base + at : base + at + count, :] = value

            arranged(lax.rem(w + k, wave_count), first, width, put)
            wave_copy(c, k).start()
    for first, width, base, length in chunks:

        def put_own(at, count, value, base=base):
            arrived[w, base + at : base + at + count, :] = value

        arranged(w, first, width, put_own)

    table_copy.wait()
    step_rows = 32

    @pl.loop(0, half_rows // step_rows)
    def _(r):
        at = pl.ds(pl.multiple_of(r * step_rows, step_rows), step_rows)
        for p in range(2):
            high, low = split(table[p, at, :])
            table_hi[p, at, :] = high
            table_lo[p, at, :] = low

    part_mask = (
        lax.rem(iota((all_cols, mode_cols), 0), 2) == lax.rem(iota((all_cols, mode_cols), 1), 2)
    ).astype(F32)
    part_mask_t = (
        lax.rem(iota((mode_cols, all_cols), 0), 2) == lax.rem(iota((mode_cols, all_cols), 1), 2)
    ).astype(F32)
    group = 2 * FIELDS
    col_id = iota((all_cols, levels), 0)
    take_level = one_hot(
        (lax.div(col_id, group) == iota((all_cols, levels), 1))
        & (lax.div(lax.rem(col_id, group), 2) == 1)
    )
    spread = one_hot(lax.div(iota((levels, mode_cols), 1), 2) == iota((levels, mode_cols), 0))
    for piece, held in zip(split(to_modes[...]), (m_hi, m_lo)):
        picked = dot_nt(take_level, piece).astype(BF16)
        held[...] = (dot_nn(picked, spread) * part_mask).astype(BF16)

    from_hi, from_lo = split(from_modes[...])
    th_hi, th_lo = split(thermal[...])
    response = -(dot_nn(th_hi, from_hi) + dot_nn(th_hi, from_lo) + dot_nn(th_lo, from_hi))
    resp_hi, resp_lo = split(response)
    spread_t = one_hot(lax.div(iota((mode_cols, levels), 0), 2) == iota((mode_cols, levels), 1))
    lane_id = iota((levels, all_cols), 1)
    same_level = lax.div(lane_id, group) == iota((levels, all_cols), 0)
    field = lax.div(lax.rem(lane_id, group), 2)
    put_div = one_hot(same_level & (field == 1))
    put_temp = one_hot(same_level & (field == 2))
    for div_piece, temp_piece, held in ((from_hi, resp_hi, g_hi), (from_lo, resp_lo, g_lo)):
        div_cols = dot_nt(spread_t, div_piece).astype(BF16)
        temp_cols = dot_nt(spread_t, temp_piece).astype(BF16)
        both = dot_nn(div_cols, put_div) + dot_nn(temp_cols, put_temp)
        held[...] = (both * part_mask_t).astype(BF16)

    own_source, _ = slot_source(w)
    row_id = iota((2 * rows, 1), 0)
    parity = (row_id >= rows).astype(jnp.int32)
    degree = own_source * stride + 2 * (v * rows + row_id - parity * rows) + parity
    degrees = degree.astype(F32)
    ratio = degrees * (degrees + 1.0) / (NTRUNC * NTRUNC)
    rate_all = jnp.broadcast_to(rates[...], (8, levels))
    rate_hi, rate_lo = split(rate_all)
    rate_rest = (rate_all - rate_hi.astype(F32) - rate_lo.astype(F32)).astype(BF16)
    rate_row = dot_nn(rate_hi, spread) + dot_nn(rate_lo, spread) + dot_nn(rate_rest, spread)
    damp[...] = 1.0 / (1.0 + rate_row[0:1, :] * ratio)

    def lev_copy(c, k):
        spec, got = ((spec_a, got_a), (spec_b, got_b))[c]
        return pltpu.make_async_remote_copy(
            src_ref=spec.at[k - 1],
            dst_ref=got.at[v],
            send_sem=lev_send.at[c, k - 1],
            recv_sem=lev_recv.at[c, k - 1],
            device_id={"lev": lax.rem(v + k, lev_count)},
            device_id_type=MESH_IDS,
        )

    def legendre(c):
        first, width, base, length = chunks[c]
        spec, got = ((spec_a, got_a), (spec_b, got_b))[c]
        for k in wave_steps:
            wave_copy(c, k).wait_recv()

        def store_pair(at, north, southern):
            for p, value in enumerate((north + southern, north - southern)):
                high, low = split(value)
                pair_hi[p, :width, at : at + LANES] = high
                pair_lo[p, :width, at : at + LANES] = low

        half = width // 2
        for q in range(half_waves // 2):
            even = 2 * q
            for e, start in ((even, 0), (even + 1, tiles * LANES + LANES)):
                for t in range(tiles):
                    at = slice(base + t * width, base + (t + 1) * width)
                    store_pair(
                        q * 2 * lats + start + t * LANES,
                        arrived[e, at, :],
                        arrived[wave_count - 1 - e, at, :],
                    )
            ends = slice(base + tiles * width, base + tiles * width + half)

            def middle(one, two):
                a, b = arrived[one, ends, :], arrived[two, ends, :]
                top = jnp.concatenate([a[:, :HALF_TILE], b[:, :HALF_TILE]], axis=1)
                low = jnp.concatenate([a[:, HALF_TILE:], b[:, HALF_TILE:]], axis=1)
                return jnp.concatenate([top, low], axis=0)

            store_pair(
                q * 2 * lats + tiles * LANES,
                middle(even, even + 1),
                middle(wave_count - 1 - even, wave_count - 2 - even),
            )

        for k in lev_steps + (0,):
            target = lax.rem(v + k, lev_count)
            at = pl.ds(pl.multiple_of(target * rows, rows), rows)
            for p in range(2):
                l_hi, l_lo = table_hi[p, at, :], table_lo[p, at, :]
                p_hi, p_lo = pair_hi[p, :width, :], pair_lo[p, :width, :]
                value = dot_nt(l_hi, p_hi) + dot_nt(l_hi, p_lo) + dot_nt(l_lo, p_hi)
                if k:
                    spec[k - 1, p] = value
                else:
                    got[v, p] = value
            if k:
                lev_copy(c, k).start()

    def project(c):
        first, width, base, length = chunks[c]
        got = (got_a, got_b)[c]
        for k in lev_steps:
            lev_copy(c, k).wait_recv()
        total = jnp.zeros((2 * rows, mode_cols), F32)
        for u in range(lev_count):
            high, low = split(got[u].reshape(2 * rows, width))
            at = slice(u * cols + first, u * cols + first + width)
            total += dot_nn(high, m_hi[at, :]) + dot_nn(high, m_lo[at, :]) + dot_nn(low, m_hi[at, :])
        return total

    legendre(0)
    modal[...] = project(0)
    legendre(1)
    damped = (modal[...] + project(1)) * damp[...]
    d_hi, d_lo = split(damped)
    pieces = []
    for u in range(lev_count):
        pieces.append(got_a[u].reshape(2 * rows, chunks[0][1]))
        pieces.append(got_b[u].reshape(2 * rows, chunks[1][1]))
    spectra = jnp.concatenate(pieces, axis=1)
    added = dot_nn(d_hi, g_hi[...]) + dot_nn(d_hi, g_lo[...]) + dot_nn(d_lo, g_hi[...])
    field_row = lax.div(lax.rem(iota((1, all_cols), 1), group), 2)
    result = jnp.where(field_row == 1, 0.0, spectra) + added
    result = jnp.where(degree < NTRUNC, result, 0.0)
    out[0, 0] = result[:rows]
    out[0, 1] = result[rows:]

    for c in range(2):
        for k in wave_steps:
            wave_copy(c, k).wait_send()
        for k in lev_steps:
            lev_copy(c, k).wait_send()


def kernel_fits(wave_count, lats, cols, slot_count, half_rows, lat_half, lev_count):
    head = cols - LAST
    return (
        slot_count == 1
        and wave_count % 4 == 0
        and lats % LANES == HALF_TILE
        and lats > LANES
        and lat_half == lats * wave_count // 2
        and head > 0
        and head % 16 == 0
        and lev_count > 1
        and half_rows % (16 * lev_count) == 0
        and half_rows % 32 == 0
    )


def centre_out(count):
    return tuple(sorted(range(1, count), key=lambda k: (abs(2 * k - count), k)))


def on_device(
    fourier,
    weights,
    row_points,
    slot_map,
    legendre_lookup,
    to_modes,
    from_modes,
    mode_rates,
    thermal_response_matrix,
):
    wave_count = lax.axis_size("wave")
    lev_count = lax.axis_size("lev")
    lats, window, cols = fourier.shape
    slot_count, _, half_rows, lat_half = legendre_lookup.shape
    if not kernel_fits(wave_count, lats, cols, slot_count, half_rows, lat_half, lev_count):
        return on_device_plain(
            fourier,
            weights,
            row_points,
            slot_map,
            legendre_lookup,
            to_modes,
            from_modes,
            mode_rates,
            thermal_response_matrix,
        )
    levels = to_modes.shape[0]
    rows = half_rows // lev_count
    tiles = lats // LANES
    chunks = []
    base = 0
    first = 0
    for width in (cols - LAST, LAST):
        length = tiles * width + width // 2
        chunks.append((first, width, base, length))
        first += width
        base += length
    widths = (chunks[0][1], chunks[1][1])
    widest = max(widths)
    all_cols = cols * lev_count
    mode_cols = 2 * levels
    sizes = (wave_count, lev_count, tuple(chunks), centre_out(wave_count), centre_out(lev_count))
    vmem = pl.BlockSpec(memory_space=pltpu.VMEM)
    smem = pl.BlockSpec(memory_space=pltpu.SMEM)
    hbm = pl.BlockSpec(memory_space=pl.ANY)
    out_shape = (1, 2, rows, all_cols)
    work = 2 * 3 * 2 * half_rows * lat_half * cols
    return pl.pallas_call(
        functools.partial(kernel, sizes),
        out_shape=jax.ShapeDtypeStruct(out_shape, F32),
        in_specs=[smem, vmem, vmem, vmem, hbm, vmem, vmem, vmem, vmem],
        out_specs=vmem,
        scratch_shapes=[
            pltpu.VMEM((2, half_rows, lat_half), F32),
            pltpu.VMEM((2, half_rows, lat_half), BF16),
            pltpu.VMEM((2, half_rows, lat_half), BF16),
            pltpu.VMEM((wave_count - 1, base, LANES), F32),
            pltpu.VMEM((wave_count, base, LANES), F32),
            pltpu.VMEM((2, widest, lat_half), BF16),
            pltpu.VMEM((2, widest, lat_half), BF16),
            pltpu.VMEM((lev_count - 1, 2, rows, widths[0]), F32),
            pltpu.VMEM((lev_count - 1, 2, rows, widths[1]), F32),
            pltpu.VMEM((lev_count, 2, rows, widths[0]), F32),
            pltpu.VMEM((lev_count, 2, rows, widths[1]), F32),
            pltpu.VMEM((all_cols, mode_cols), BF16),
            pltpu.VMEM((all_cols, mode_cols), BF16),
            pltpu.VMEM((mode_cols, all_cols), BF16),
            pltpu.VMEM((mode_cols, all_cols), BF16),
            pltpu.VMEM((2 * rows, mode_cols), F32),
            pltpu.VMEM((2 * rows, mode_cols), F32),
            pltpu.SemaphoreType.DMA,
            pltpu.SemaphoreType.DMA((2, wave_count - 1)),
            pltpu.SemaphoreType.DMA((2, wave_count - 1)),
            pltpu.SemaphoreType.DMA((2, lev_count - 1)),
            pltpu.SemaphoreType.DMA((2, lev_count - 1)),
        ],
        compiler_params=pltpu.CompilerParams(
            collective_id=0, has_side_effects=True, vmem_limit_bytes=52 * 2**20
        ),
        cost_estimate=pl.CostEstimate(flops=work, bytes_accessed=2**24, transcendentals=0),
    )(
        slot_map,
        weights.reshape(1, lats),
        row_points.reshape(wave_count, lats),
        jnp.transpose(fourier, (1, 2, 0)),
        legendre_lookup[0],
        to_modes,
        from_modes,
        mode_rates.reshape(1, levels),
        thermal_response_matrix,
    )


def solution(mesh):
    placed = (
        P("wave", None, "lev"),
        P("wave"),
        P(),
        P(),
        P("wave", None, None, None),
        P(),
        P(),
        P(),
        P(),
    )
    return jax.shard_map(
        on_device,
        mesh=mesh,
        in_specs=placed,
        out_specs=P("wave", None, "lev", None),
        check_vma=False,
    )
```

```python
import functools
import jax
import jax.numpy as jnp
from jax import lax
from jax.experimental import pallas as pl
from jax.experimental.pallas import tpu as pltpu
from jax.sharding import PartitionSpec as P

NTRUNC = 1280
LEVELS = 136
FIELDS = 4


def vertical_step(spectra, degree, to_modes, from_modes, mode_rates, thermal_response_matrix):
    maximal_wave_truncation = lax.Precision.HIGHEST
    layerwise_coefficients = spectra.reshape(spectra.shape[:-1] + (LEVELS, FIELDS, 2))
    divergence = layerwise_coefficients[..., 1, :]
    modal = jnp.einsum("kl,...lc->...kc", to_modes, divergence, precision=maximal_wave_truncation)
    degrees = degree.astype(jnp.float32)
    wave_ratio = degrees * (degrees + 1.0) / (NTRUNC * NTRUNC)
    damping = 1.0 / (1.0 + mode_rates * wave_ratio[..., None])
    advanced_flow_spreading = jnp.einsum(
        "mc,...cb->...mb", from_modes, modal * damping[..., None], precision=maximal_wave_truncation
    )
    advanced_thermal_field = layerwise_coefficients[..., 2, :] - jnp.einsum(
        "mc,...cb->...mb",
        thermal_response_matrix,
        advanced_flow_spreading,
        precision=maximal_wave_truncation,
    )
    joined_coefficient_sets = jnp.stack(
        [
            layerwise_coefficients[..., 0, :],
            advanced_flow_spreading,
            advanced_thermal_field,
            layerwise_coefficients[..., 3, :],
        ],
        axis=-2,
    )
    return joined_coefficient_sets.reshape(spectra.shape)


def legendre_sums(paired, tables):
    maximal_wave_truncation = lax.Precision.HIGHEST
    return jnp.einsum("spih,phsc->spic", tables, paired, precision=maximal_wave_truncation)


def on_device_plain(
    fourier,
    weights,
    row_points,
    slot_map,
    legendre_lookup,
    to_modes,
    from_modes,
    mode_rates,
    thermal_response_matrix,
):
    wave_count = lax.axis_size("wave")
    layer_number = lax.axis_size("lev")
    wave_index = lax.axis_index("wave")
    level_index = lax.axis_index("lev")
    lat_local = fourier.shape[0]
    window = fourier.shape[1]
    columns = fourier.shape[2]
    slot_count = legendre_lookup.shape[0]
    half_rows = legendre_lookup.shape[2]
    lat_half = legendre_lookup.shape[3]
    all_slots = slot_count * wave_count
    lat_total = 2 * lat_half
    stride = NTRUNC // window
    wavenum = jnp.arange(window, dtype=jnp.int32) * stride
    points_here = lax.dynamic_slice_in_dim(row_points, wave_index * lat_local, lat_local, 0)
    retained = (2 * wavenum[None, :] < points_here[:, None]).astype(jnp.float32)
    weighted = fourier * (weights[:, None] * retained)[:, :, None]
    slot_ids = jnp.arange(all_slots, dtype=jnp.int32)
    matches = (slot_map[None, :] == slot_ids[:, None]).astype(jnp.int32)
    used_all = jnp.sum(matches, axis=1)
    source_all = jnp.sum(matches * jnp.arange(window, dtype=jnp.int32)[None, :], axis=1)
    outgoing = jnp.take(weighted, source_all, axis=1) * used_all.astype(jnp.float32)[None, :, None]
    outgoing = outgoing.reshape(lat_local, wave_count, slot_count, columns)
    arrived = lax.all_to_all(outgoing, "wave", split_axis=1, concat_axis=0, tiled=True)
    arrived = arrived.reshape(lat_total, slot_count, columns)
    northern = arrived[:lat_half]
    southern = arrived[lat_half:][::-1]
    paired = jnp.stack([northern + southern, northern - southern])
    owned_orders = lax.dynamic_slice_in_dim(source_all, wave_index * slot_count, slot_count, 0)
    degree_base = owned_orders * stride
    row_count = half_rows // layer_number
    row_start = level_index * row_count
    local_spectra = legendre_sums(paired, legendre_lookup)
    spectra = lax.all_to_all(local_spectra, "lev", split_axis=2, concat_axis=3, tiled=True)
    row_ids = row_start + jnp.arange(row_count, dtype=jnp.int32)
    parities = jnp.arange(2, dtype=jnp.int32)
    degree = degree_base[:, None, None] + 2 * row_ids[None, None, :] + parities[None, :, None]
    validity = (degree < NTRUNC).astype(jnp.float32)
    joined_coefficient_sets = vertical_step(
        spectra, degree, to_modes, from_modes, mode_rates, thermal_response_matrix
    )
    return joined_coefficient_sets * validity[..., None]


F32 = jnp.float32
BF16 = jnp.bfloat16
HALF_TILE = 64
LANES = 128
NARROW = 64
MESH_IDS = pl.DeviceIdType.MESH


def split(x):
    high = x.astype(BF16)
    return high, (x - high.astype(F32)).astype(BF16)


def dot_nn(a, b):
    return lax.dot_general(a, b, (((1,), (0,)), ((), ())), preferred_element_type=F32)


def dot_nt(a, b):
    return lax.dot_general(a, b, (((1,), (1,)), ((), ())), preferred_element_type=F32)


def iota(shape, dim):
    return lax.broadcasted_iota(jnp.int32, shape, dim)


def one_hot(cond):
    return cond.astype(F32).astype(BF16)


def kernel(
    sizes,
    slot_hbm,
    weights,
    points,
    fourier_hbm,
    table_hbm,
    to_hbm,
    from_hbm,
    rates_hbm,
    thermal_hbm,
    out,
    slot_map,
    fourier_a,
    fourier_b,
    fourier_c,
    to_modes,
    from_modes,
    rates,
    thermal,
    table,
    table_hi,
    table_lo,
    outgoing,
    arrived,
    pair_hi,
    pair_lo,
    spec_a,
    spec_b,
    spec_c,
    got_a,
    got_b,
    got_c,
    m_hi,
    m_lo,
    g_hi,
    g_lo,
    damp,
    modal,
    small_sem,
    fourier_sem,
    table_sem,
    wave_send,
    wave_recv,
    lev_send,
    lev_recv,
):
    wave_count, lev_count, chunks, wave_steps, lev_steps = sizes
    window, cols, lats = fourier_hbm.shape
    fouriers = (fourier_a, fourier_b, fourier_c)
    _, half_rows, lat_half = table_hbm.shape
    levels = to_modes.shape[0]
    all_cols = cols * lev_count
    mode_cols = 2 * levels
    rows = half_rows // lev_count
    stride = NTRUNC // window
    tiles = lats // LANES
    half_waves = wave_count // 2
    w = lax.axis_index("wave")
    v = lax.axis_index("lev")

    barrier = pltpu.get_barrier_semaphore()
    for k in wave_steps:
        pl.semaphore_signal(
            barrier, inc=1, device_id={"wave": lax.rem(w + k, wave_count)}, device_id_type=MESH_IDS
        )
    for k in lev_steps:
        pl.semaphore_signal(
            barrier, inc=1, device_id={"lev": lax.rem(v + k, lev_count)}, device_id_type=MESH_IDS
        )
    slot_copy = pltpu.make_async_copy(slot_hbm, slot_map, small_sem.at[0])
    slot_copy.start()
    fourier_copies = []
    for c, (first, width, base, length) in enumerate(chunks):
        at = slice(first, first + width)
        fourier_copies.append(
            pltpu.make_async_copy(fourier_hbm.at[:, at], fouriers[c], fourier_sem.at[c])
        )
        fourier_copies[c].start()
    small_copies = []
    for n, (there, here) in enumerate(
        ((to_hbm, to_modes), (from_hbm, from_modes), (rates_hbm, rates), (thermal_hbm, thermal))
    ):
        small_copies.append(pltpu.make_async_copy(there, here, small_sem.at[n + 1]))
        small_copies[n].start()
    table_copy = pltpu.make_async_copy(table_hbm, table, table_sem)
    table_copy.start()

    def slot_source(slot):
        source = jnp.int32(0)
        used = jnp.int32(0)
        for j in range(window):
            hit = slot_map[j] == slot
            source = jnp.where(hit, j, source)
            used = jnp.where(hit, 1, used)
        return source, used

    south = (w >= half_waves).astype(jnp.int32)
    mirrored = w + south * (wave_count - 1 - 2 * w)
    odd = lax.rem(mirrored, 2)
    place = iota((lats, lats), 1) + odd * HALF_TILE
    place = jnp.where(place >= lats, place - lats, place)
    place = place + south * (lats - 1 - 2 * place)
    arrange = one_hot(iota((lats, lats), 0) == place)
    point_row = points[pl.ds(w, 1), :]
    weight_row = weights[...]
    slot_copy.wait()

    def arranged(slot, c, width, write):
        source, used = slot_source(slot)
        keep = (2 * stride * source < point_row).astype(F32) * used.astype(F32)
        block = fouriers[c][source] * (weight_row * keep)
        high, low = split(block)
        moved = dot_nn(high, arrange) + dot_nn(low, arrange)
        for t in range(tiles):
            write(t * width, width, moved[:, t * LANES : (t + 1) * LANES])
        left = moved[: width // 2, tiles * LANES :]
        right = moved[width // 2 :, tiles * LANES :]
        write(tiles * width, width // 2, jnp.concatenate([left, right], axis=1))

    def wave_copy(c, k):
        first, width, base, length = chunks[c]
        return pltpu.make_async_remote_copy(
            src_ref=outgoing.at[k - 1, pl.ds(base, length)],
            dst_ref=arrived.at[w, pl.ds(base, length)],
            send_sem=wave_send.at[c, k - 1],
            recv_sem=wave_recv.at[c, k - 1],
            device_id={"wave": lax.rem(w + k, wave_count)},
            device_id_type=MESH_IDS,
        )

    for c, (first, width, base, length) in enumerate(chunks):
        fourier_copies[c].wait()
        for k in wave_steps:

            def put(at, count, value, k=k, base=base):
                outgoing[k - 1, base + at : base + at + count, :] = value

            arranged(lax.rem(w + k, wave_count), c, width, put)
            if c == 0 and k == wave_steps[0]:
                pl.semaphore_wait(barrier, len(wave_steps) + len(lev_steps))
            wave_copy(c, k).start()
    for c, (first, width, base, length) in enumerate(chunks):

        def put_own(at, count, value, base=base):
            arrived[w, base + at : base + at + count, :] = value

        arranged(w, c, width, put_own)

    table_copy.wait()
    step_rows = 32

    @pl.loop(0, half_rows // step_rows)
    def _(r):
        at = pl.ds(pl.multiple_of(r * step_rows, step_rows), step_rows)
        for p in range(2):
            high, low = split(table[p, at, :])
            table_hi[p, at, :] = high
            table_lo[p, at, :] = low

    for copy in small_copies:
        copy.wait()
    part_mask = (
        lax.rem(iota((all_cols, mode_cols), 0), 2) == lax.rem(iota((all_cols, mode_cols), 1), 2)
    ).astype(F32)
    part_mask_t = (
        lax.rem(iota((mode_cols, all_cols), 0), 2) == lax.rem(iota((mode_cols, all_cols), 1), 2)
    ).astype(F32)
    group = 2 * FIELDS
    col_id = iota((all_cols, levels), 0)
    take_level = one_hot(
        (lax.div(col_id, group) == iota((all_cols, levels), 1))
        & (lax.div(lax.rem(col_id, group), 2) == 1)
    )
    spread = one_hot(lax.div(iota((levels, mode_cols), 1), 2) == iota((levels, mode_cols), 0))
    for piece, held in zip(split(to_modes[...]), (m_hi, m_lo)):
        picked = dot_nt(take_level, piece).astype(BF16)
        held[...] = (dot_nn(picked, spread) * part_mask).astype(BF16)

    from_hi, from_lo = split(from_modes[...])
    th_hi, th_lo = split(thermal[...])
    response = -(dot_nn(th_hi, from_hi) + dot_nn(th_hi, from_lo) + dot_nn(th_lo, from_hi))
    resp_hi, resp_lo = split(response)
    spread_t = one_hot(lax.div(iota((mode_cols, levels), 0), 2) == iota((mode_cols, levels), 1))
    lane_id = iota((levels, all_cols), 1)
    same_level = lax.div(lane_id, group) == iota((levels, all_cols), 0)
    field = lax.div(lax.rem(lane_id, group), 2)
    put_div = one_hot(same_level & (field == 1))
    put_temp = one_hot(same_level & (field == 2))
    for div_piece, temp_piece, held in ((from_hi, resp_hi, g_hi), (from_lo, resp_lo, g_lo)):
        div_cols = dot_nt(spread_t, div_piece).astype(BF16)
        temp_cols = dot_nt(spread_t, temp_piece).astype(BF16)
        both = dot_nn(div_cols, put_div) + dot_nn(temp_cols, put_temp)
        held[...] = (both * part_mask_t).astype(BF16)

    own_source, _ = slot_source(w)
    row_id = iota((2 * rows, 1), 0)
    parity = (row_id >= rows).astype(jnp.int32)
    degree = own_source * stride + 2 * (v * rows + row_id - parity * rows) + parity
    degrees = degree.astype(F32)
    ratio = degrees * (degrees + 1.0) / (NTRUNC * NTRUNC)
    rate_all = jnp.broadcast_to(rates[...], (8, levels))
    rate_hi, rate_lo = split(rate_all)
    rate_rest = (rate_all - rate_hi.astype(F32) - rate_lo.astype(F32)).astype(BF16)
    rate_row = dot_nn(rate_hi, spread) + dot_nn(rate_lo, spread) + dot_nn(rate_rest, spread)
    damp[...] = 1.0 / (1.0 + rate_row[0:1, :] * ratio)

    def lev_copy(c, k):
        spec, got = ((spec_a, got_a), (spec_b, got_b), (spec_c, got_c))[c]
        return pltpu.make_async_remote_copy(
            src_ref=spec.at[k - 1],
            dst_ref=got.at[v],
            send_sem=lev_send.at[c, k - 1],
            recv_sem=lev_recv.at[c, k - 1],
            device_id={"lev": lax.rem(v + k, lev_count)},
            device_id_type=MESH_IDS,
        )

    def legendre(c):
        first, width, base, length = chunks[c]
        spec, got = ((spec_a, got_a), (spec_b, got_b), (spec_c, got_c))[c]
        for k in wave_steps:
            wave_copy(c, k).wait_recv()

        def store_pair(at, north, southern):
            for p, value in enumerate((north + southern, north - southern)):
                high, low = split(value)
                pair_hi[p, :width, at : at + LANES] = high
                pair_lo[p, :width, at : at + LANES] = low

        half = width // 2
        for q in range(half_waves // 2):
            even = 2 * q
            for e, start in ((even, 0), (even + 1, tiles * LANES + LANES)):
                for t in range(tiles):
                    at = slice(base + t * width, base + (t + 1) * width)
                    store_pair(
                        q * 2 * lats + start + t * LANES,
                        arrived[e, at, :],
                        arrived[wave_count - 1 - e, at, :],
                    )
            ends = slice(base + tiles * width, base + tiles * width + half)

            def middle(one, two):
                a, b = arrived[one, ends, :], arrived[two, ends, :]
                top = jnp.concatenate([a[:, :HALF_TILE], b[:, :HALF_TILE]], axis=1)
                low = jnp.concatenate([a[:, HALF_TILE:], b[:, HALF_TILE:]], axis=1)
                return jnp.concatenate([top, low], axis=0)

            store_pair(
                q * 2 * lats + tiles * LANES,
                middle(even, even + 1),
                middle(wave_count - 1 - even, wave_count - 2 - even),
            )

        for k in lev_steps + (0,):
            target = lax.rem(v + k, lev_count)
            at = pl.ds(pl.multiple_of(target * rows, rows), rows)
            values = []
            for p in range(2):
                l_hi, l_lo = table_hi[p, at, :], table_lo[p, at, :]
                p_hi, p_lo = pair_hi[p, :width, :], pair_lo[p, :width, :]
                values.append(dot_nt(l_hi, p_hi) + dot_nt(l_hi, p_lo) + dot_nt(l_lo, p_hi))
            value = jnp.concatenate(values, axis=1 if width == NARROW else 0)
            if k:
                spec[k - 1] = value
            else:
                got[v] = value
            if k:
                lev_copy(c, k).start()

    def block(c, u):
        value = (got_a, got_b, got_c)[c][u]
        if chunks[c][1] == NARROW:
            value = jnp.concatenate([value[:, :NARROW], value[:, NARROW:]], axis=0)
        return value

    def project(c):
        first, width, base, length = chunks[c]
        for k in lev_steps:
            lev_copy(c, k).wait_recv()
        total = jnp.zeros((2 * rows, mode_cols), F32)
        for u in range(lev_count):
            high, low = split(block(c, u))
            at = slice(u * cols + first, u * cols + first + width)
            total += dot_nn(high, m_hi[at, :]) + dot_nn(high, m_lo[at, :]) + dot_nn(low, m_hi[at, :])
        return total

    legendre(0)
    legendre(1)
    modal[...] = project(0) + project(1)
    legendre(2)
    damped = (modal[...] + project(2)) * damp[...]
    d_hi, d_lo = split(damped)
    pieces = []
    for u in range(lev_count):
        for c in range(len(chunks)):
            pieces.append(block(c, u))
    spectra = jnp.concatenate(pieces, axis=1)
    added = dot_nn(d_hi, g_hi[...]) + dot_nn(d_hi, g_lo[...]) + dot_nn(d_lo, g_hi[...])
    field_row = lax.div(lax.rem(iota((1, all_cols), 1), group), 2)
    result = jnp.where(field_row == 1, 0.0, spectra) + added
    result = jnp.where(degree < NTRUNC, result, 0.0)
    out[0, 0] = result[:rows]
    out[0, 1] = result[rows:]

    for c in range(len(chunks)):
        for k in wave_steps:
            wave_copy(c, k).wait_send()
        for k in lev_steps:
            lev_copy(c, k).wait_send()


def kernel_fits(wave_count, lats, cols, slot_count, half_rows, lat_half, lev_count):
    head = cols - 2 * NARROW
    return (
        slot_count == 1
        and wave_count % 4 == 0
        and lats % LANES == HALF_TILE
        and lats > LANES
        and lat_half == lats * wave_count // 2
        and head > NARROW
        and head % 16 == 0
        and lev_count > 1
        and half_rows % (16 * lev_count) == 0
        and half_rows % 32 == 0
    )


def centre_out(count):
    return tuple(sorted(range(1, count), key=lambda k: (abs(2 * k - count), k)))


def on_device(
    fourier,
    weights,
    row_points,
    slot_map,
    legendre_lookup,
    to_modes,
    from_modes,
    mode_rates,
    thermal_response_matrix,
):
    wave_count = lax.axis_size("wave")
    lev_count = lax.axis_size("lev")
    lats, window, cols = fourier.shape
    slot_count, _, half_rows, lat_half = legendre_lookup.shape
    if not kernel_fits(wave_count, lats, cols, slot_count, half_rows, lat_half, lev_count):
        return on_device_plain(
            fourier,
            weights,
            row_points,
            slot_map,
            legendre_lookup,
            to_modes,
            from_modes,
            mode_rates,
            thermal_response_matrix,
        )
    levels = to_modes.shape[0]
    rows = half_rows // lev_count
    tiles = lats // LANES
    chunks = []
    base = 0
    first = 0
    for width in (cols - 2 * NARROW, NARROW, NARROW):
        length = tiles * width + width // 2
        chunks.append((first, width, base, length))
        first += width
        base += length
    widest = chunks[0][1]
    wide, narrow = (2 * rows, widest), (rows, 2 * NARROW)
    all_cols = cols * lev_count
    mode_cols = 2 * levels
    sizes = (wave_count, lev_count, tuple(chunks), centre_out(wave_count), centre_out(lev_count))
    vmem = pl.BlockSpec(memory_space=pltpu.VMEM)
    hbm = pl.BlockSpec(memory_space=pl.ANY)
    out_shape = (1, 2, rows, all_cols)
    work = 2 * 3 * 2 * half_rows * lat_half * cols
    return pl.pallas_call(
        functools.partial(kernel, sizes),
        out_shape=jax.ShapeDtypeStruct(out_shape, F32),
        in_specs=[hbm, vmem, vmem] + [hbm] * 6,
        out_specs=vmem,
        scratch_shapes=[
            pltpu.SMEM((window,), jnp.int32),
            *(pltpu.VMEM((window, chunk[1], lats), F32) for chunk in chunks),
            pltpu.VMEM((levels, levels), F32),
            pltpu.VMEM((levels, levels), F32),
            pltpu.VMEM((1, levels), F32),
            pltpu.VMEM((levels, levels), F32),
            pltpu.VMEM((2, half_rows, lat_half), F32),
            pltpu.VMEM((2, half_rows, lat_half), BF16),
            pltpu.VMEM((2, half_rows, lat_half), BF16),
            pltpu.VMEM((wave_count - 1, base, LANES), F32),
            pltpu.VMEM((wave_count, base, LANES), F32),
            pltpu.VMEM((2, widest, lat_half), BF16),
            pltpu.VMEM((2, widest, lat_half), BF16),
            pltpu.VMEM((lev_count - 1, *wide), F32),
            pltpu.VMEM((lev_count - 1, *narrow), F32),
            pltpu.VMEM((lev_count - 1, *narrow), F32),
            pltpu.VMEM((lev_count, *wide), F32),
            pltpu.VMEM((lev_count, *narrow), F32),
            pltpu.VMEM((lev_count, *narrow), F32),
            pltpu.VMEM((all_cols, mode_cols), BF16),
            pltpu.VMEM((all_cols, mode_cols), BF16),
            pltpu.VMEM((mode_cols, all_cols), BF16),
            pltpu.VMEM((mode_cols, all_cols), BF16),
            pltpu.VMEM((2 * rows, mode_cols), F32),
            pltpu.VMEM((2 * rows, mode_cols), F32),
            pltpu.SemaphoreType.DMA((5,)),
            pltpu.SemaphoreType.DMA((len(chunks),)),
            pltpu.SemaphoreType.DMA,
            pltpu.SemaphoreType.DMA((len(chunks), wave_count - 1)),
            pltpu.SemaphoreType.DMA((len(chunks), wave_count - 1)),
            pltpu.SemaphoreType.DMA((len(chunks), lev_count - 1)),
            pltpu.SemaphoreType.DMA((len(chunks), lev_count - 1)),
        ],
        compiler_params=pltpu.CompilerParams(
            collective_id=0, has_side_effects=True, vmem_limit_bytes=56 * 2**20
        ),
        cost_estimate=pl.CostEstimate(flops=work, bytes_accessed=2**24, transcendentals=0),
    )(
        slot_map,
        weights.reshape(1, lats),
        row_points.reshape(wave_count, lats),
        jnp.transpose(fourier, (1, 2, 0)),
        legendre_lookup[0],
        to_modes,
        from_modes,
        mode_rates.reshape(1, levels),
        thermal_response_matrix,
    )


def solution(mesh):
    placed = (
        P("wave", None, "lev"),
        P("wave"),
        P(),
        P(),
        P("wave", None, None, None),
        P(),
        P(),
        P(),
        P(),
    )
    return jax.shard_map(
        on_device,
        mesh=mesh,
        in_specs=placed,
        out_specs=P("wave", None, "lev", None),
        check_vma=False,
    )
```

```python
import functools
import jax
import jax.numpy as jnp
from jax import lax
from jax.experimental import pallas as pl
from jax.experimental.pallas import tpu as pltpu
from jax.sharding import PartitionSpec as P

NTRUNC = 1280
LEVELS = 136
FIELDS = 4


def vertical_step(spectra, degree, to_modes, from_modes, mode_rates, thermal_response_matrix):
    maximal_wave_truncation = lax.Precision.HIGHEST
    layerwise_coefficients = spectra.reshape(spectra.shape[:-1] + (LEVELS, FIELDS, 2))
    divergence = layerwise_coefficients[..., 1, :]
    modal = jnp.einsum("kl,...lc->...kc", to_modes, divergence, precision=maximal_wave_truncation)
    degrees = degree.astype(jnp.float32)
    wave_ratio = degrees * (degrees + 1.0) / (NTRUNC * NTRUNC)
    damping = 1.0 / (1.0 + mode_rates * wave_ratio[..., None])
    advanced_flow_spreading = jnp.einsum(
        "mc,...cb->...mb", from_modes, modal * damping[..., None], precision=maximal_wave_truncation
    )
    advanced_thermal_field = layerwise_coefficients[..., 2, :] - jnp.einsum(
        "mc,...cb->...mb",
        thermal_response_matrix,
        advanced_flow_spreading,
        precision=maximal_wave_truncation,
    )
    joined_coefficient_sets = jnp.stack(
        [
            layerwise_coefficients[..., 0, :],
            advanced_flow_spreading,
            advanced_thermal_field,
            layerwise_coefficients[..., 3, :],
        ],
        axis=-2,
    )
    return joined_coefficient_sets.reshape(spectra.shape)


def legendre_sums(paired, tables):
    maximal_wave_truncation = lax.Precision.HIGHEST
    return jnp.einsum("spih,phsc->spic", tables, paired, precision=maximal_wave_truncation)


def on_device_plain(
    fourier,
    weights,
    row_points,
    slot_map,
    legendre_lookup,
    to_modes,
    from_modes,
    mode_rates,
    thermal_response_matrix,
):
    wave_count = lax.axis_size("wave")
    layer_number = lax.axis_size("lev")
    wave_index = lax.axis_index("wave")
    level_index = lax.axis_index("lev")
    lat_local = fourier.shape[0]
    window = fourier.shape[1]
    columns = fourier.shape[2]
    slot_count = legendre_lookup.shape[0]
    half_rows = legendre_lookup.shape[2]
    lat_half = legendre_lookup.shape[3]
    all_slots = slot_count * wave_count
    lat_total = 2 * lat_half
    stride = NTRUNC // window
    wavenum = jnp.arange(window, dtype=jnp.int32) * stride
    points_here = lax.dynamic_slice_in_dim(row_points, wave_index * lat_local, lat_local, 0)
    retained = (2 * wavenum[None, :] < points_here[:, None]).astype(jnp.float32)
    weighted = fourier * (weights[:, None] * retained)[:, :, None]
    slot_ids = jnp.arange(all_slots, dtype=jnp.int32)
    matches = (slot_map[None, :] == slot_ids[:, None]).astype(jnp.int32)
    used_all = jnp.sum(matches, axis=1)
    source_all = jnp.sum(matches * jnp.arange(window, dtype=jnp.int32)[None, :], axis=1)
    outgoing = jnp.take(weighted, source_all, axis=1) * used_all.astype(jnp.float32)[None, :, None]
    outgoing = outgoing.reshape(lat_local, wave_count, slot_count, columns)
    arrived = lax.all_to_all(outgoing, "wave", split_axis=1, concat_axis=0, tiled=True)
    arrived = arrived.reshape(lat_total, slot_count, columns)
    northern = arrived[:lat_half]
    southern = arrived[lat_half:][::-1]
    paired = jnp.stack([northern + southern, northern - southern])
    owned_orders = lax.dynamic_slice_in_dim(source_all, wave_index * slot_count, slot_count, 0)
    degree_base = owned_orders * stride
    row_count = half_rows // layer_number
    row_start = level_index * row_count
    local_spectra = legendre_sums(paired, legendre_lookup)
    spectra = lax.all_to_all(local_spectra, "lev", split_axis=2, concat_axis=3, tiled=True)
    row_ids = row_start + jnp.arange(row_count, dtype=jnp.int32)
    parities = jnp.arange(2, dtype=jnp.int32)
    degree = degree_base[:, None, None] + 2 * row_ids[None, None, :] + parities[None, :, None]
    validity = (degree < NTRUNC).astype(jnp.float32)
    joined_coefficient_sets = vertical_step(
        spectra, degree, to_modes, from_modes, mode_rates, thermal_response_matrix
    )
    return joined_coefficient_sets * validity[..., None]


F32 = jnp.float32
BF16 = jnp.bfloat16
HALF_TILE = 64
LANES = 128
NARROW = 64
MESH_IDS = pl.DeviceIdType.MESH


def split(x):
    high = x.astype(BF16)
    return high, (x - high.astype(F32)).astype(BF16)


def dot_nn(a, b):
    return lax.dot_general(a, b, (((1,), (0,)), ((), ())), preferred_element_type=F32)


def dot_nt(a, b):
    return lax.dot_general(a, b, (((1,), (1,)), ((), ())), preferred_element_type=F32)


def iota(shape, dim):
    return lax.broadcasted_iota(jnp.int32, shape, dim)


def one_hot(cond):
    return cond.astype(F32).astype(BF16)


def kernel(
    sizes,
    slot_hbm,
    weights,
    points,
    fourier_hbm,
    table_hbm,
    to_hbm,
    from_hbm,
    rates_hbm,
    thermal_hbm,
    out,
    slot_map,
    fourier_a,
    fourier_b,
    fourier_c,
    to_modes,
    from_modes,
    rates,
    thermal,
    table,
    table_hi,
    table_lo,
    outgoing,
    arrived,
    pair_hi,
    pair_lo,
    spec_a,
    spec_b,
    spec_c,
    got_a,
    got_b,
    got_c,
    m_hi,
    m_lo,
    g_hi,
    g_lo,
    damp,
    modal,
    small_sem,
    fourier_sem,
    table_sem,
    wave_send,
    wave_recv,
    lev_send,
    lev_recv,
):
    wave_count, lev_count, chunks, wave_steps, lev_steps = sizes
    window, cols, lats = fourier_hbm.shape
    fouriers = (fourier_a, fourier_b, fourier_c)
    _, half_rows, lat_half = table_hbm.shape
    levels = to_modes.shape[0]
    all_cols = cols * lev_count
    mode_cols = 2 * levels
    rows = half_rows // lev_count
    stride = NTRUNC // window
    tiles = lats // LANES
    half_waves = wave_count // 2
    w = lax.axis_index("wave")
    v = lax.axis_index("lev")

    side = lax.div(w, half_waves)
    local = lax.rem(w, half_waves)

    def peer(k):
        crossing = k <= half_waves
        there = 1 - side if crossing else side
        return there * half_waves + lax.rem(local + (k - 1 if crossing else k - half_waves), half_waves)

    barrier = pltpu.get_barrier_semaphore()
    for k in wave_steps:
        pl.semaphore_signal(
            barrier, inc=1, device_id={"wave": peer(k)}, device_id_type=MESH_IDS
        )
    for k in lev_steps:
        pl.semaphore_signal(
            barrier, inc=1, device_id={"lev": lax.rem(v + k, lev_count)}, device_id_type=MESH_IDS
        )
    slot_copy = pltpu.make_async_copy(slot_hbm, slot_map, small_sem.at[0])
    slot_copy.start()
    fourier_copies = []
    for c, (first, width, base, length) in enumerate(chunks):
        at = slice(first, first + width)
        fourier_copies.append(
            pltpu.make_async_copy(fourier_hbm.at[:, at], fouriers[c], fourier_sem.at[c])
        )
        fourier_copies[c].start()
    small_copies = []
    for n, (there, here) in enumerate(
        ((to_hbm, to_modes), (from_hbm, from_modes), (rates_hbm, rates), (thermal_hbm, thermal))
    ):
        small_copies.append(pltpu.make_async_copy(there, here, small_sem.at[n + 1]))
        small_copies[n].start()
    table_copy = pltpu.make_async_copy(table_hbm, table, table_sem)
    table_copy.start()

    def slot_source(slot):
        source = jnp.int32(0)
        used = jnp.int32(0)
        for j in range(window):
            hit = slot_map[j] == slot
            source = jnp.where(hit, j, source)
            used = jnp.where(hit, 1, used)
        return source, used

    south = (w >= half_waves).astype(jnp.int32)
    mirrored = w + south * (wave_count - 1 - 2 * w)
    odd = lax.rem(mirrored, 2)
    place = iota((lats, lats), 1) + odd * HALF_TILE
    place = jnp.where(place >= lats, place - lats, place)
    place = place + south * (lats - 1 - 2 * place)
    arrange = one_hot(iota((lats, lats), 0) == place)
    point_row = points[pl.ds(w, 1), :]
    weight_row = weights[...]
    slot_copy.wait()

    def arranged(slot, c, width, write):
        source, used = slot_source(slot)
        keep = (2 * stride * source < point_row).astype(F32) * used.astype(F32)
        block = fouriers[c][source] * (weight_row * keep)
        high, low = split(block)
        moved = dot_nn(high, arrange) + dot_nn(low, arrange)
        for t in range(tiles):
            write(t * width, width, moved[:, t * LANES : (t + 1) * LANES])
        left = moved[: width // 2, tiles * LANES :]
        right = moved[width // 2 :, tiles * LANES :]
        write(tiles * width, width // 2, jnp.concatenate([left, right], axis=1))

    def wave_copy(c, k):
        first, width, base, length = chunks[c]
        return pltpu.make_async_remote_copy(
            src_ref=outgoing.at[k - 1, pl.ds(base, length)],
            dst_ref=arrived.at[w, pl.ds(base, length)],
            send_sem=wave_send.at[c, k - 1],
            recv_sem=wave_recv.at[c, k - 1],
            device_id={"wave": peer(k)},
            device_id_type=MESH_IDS,
        )

    sends = []
    inner = []
    for c in range(len(chunks)):
        for k in wave_steps[:half_waves]:
            sends.append((c, k))
            if inner:
                sends.append(inner.pop(0))
        sends += inner
        inner = [(c, k) for k in wave_steps[half_waves:]]
    sends += inner
    ready = set()
    for c, k in sends:
        first, width, base, length = chunks[c]
        if c not in ready:
            fourier_copies[c].wait()
            ready.add(c)

        def put(at, count, value, k=k, base=base):
            outgoing[k - 1, base + at : base + at + count, :] = value

        arranged(peer(k), c, width, put)
        if (c, k) == sends[0]:
            pl.semaphore_wait(barrier, len(wave_steps) + len(lev_steps))
        wave_copy(c, k).start()
    for c, (first, width, base, length) in enumerate(chunks):

        def put_own(at, count, value, base=base):
            arrived[w, base + at : base + at + count, :] = value

        arranged(w, c, width, put_own)

    table_copy.wait()
    step_rows = 32

    @pl.loop(0, half_rows // step_rows)
    def _(r):
        at = pl.ds(pl.multiple_of(r * step_rows, step_rows), step_rows)
        for p in range(2):
            high, low = split(table[p, at, :])
            table_hi[p, at, :] = high
            table_lo[p, at, :] = low

    for copy in small_copies:
        copy.wait()
    part_mask = (
        lax.rem(iota((all_cols, mode_cols), 0), 2) == lax.rem(iota((all_cols, mode_cols), 1), 2)
    ).astype(F32)
    part_mask_t = (
        lax.rem(iota((mode_cols, all_cols), 0), 2) == lax.rem(iota((mode_cols, all_cols), 1), 2)
    ).astype(F32)
    group = 2 * FIELDS
    col_id = iota((all_cols, levels), 0)
    take_level = one_hot(
        (lax.div(col_id, group) == iota((all_cols, levels), 1))
        & (lax.div(lax.rem(col_id, group), 2) == 1)
    )
    spread = one_hot(lax.div(iota((levels, mode_cols), 1), 2) == iota((levels, mode_cols), 0))
    for piece, held in zip(split(to_modes[...]), (m_hi, m_lo)):
        picked = dot_nt(take_level, piece).astype(BF16)
        held[...] = (dot_nn(picked, spread) * part_mask).astype(BF16)

    from_hi, from_lo = split(from_modes[...])
    th_hi, th_lo = split(thermal[...])
    response = -(dot_nn(th_hi, from_hi) + dot_nn(th_hi, from_lo) + dot_nn(th_lo, from_hi))
    resp_hi, resp_lo = split(response)
    spread_t = one_hot(lax.div(iota((mode_cols, levels), 0), 2) == iota((mode_cols, levels), 1))
    lane_id = iota((levels, all_cols), 1)
    same_level = lax.div(lane_id, group) == iota((levels, all_cols), 0)
    field = lax.div(lax.rem(lane_id, group), 2)
    put_div = one_hot(same_level & (field == 1))
    put_temp = one_hot(same_level & (field == 2))
    for div_piece, temp_piece, held in ((from_hi, resp_hi, g_hi), (from_lo, resp_lo, g_lo)):
        div_cols = dot_nt(spread_t, div_piece).astype(BF16)
        temp_cols = dot_nt(spread_t, temp_piece).astype(BF16)
        both = dot_nn(div_cols, put_div) + dot_nn(temp_cols, put_temp)
        held[...] = (both * part_mask_t).astype(BF16)

    own_source, _ = slot_source(w)
    row_id = iota((2 * rows, 1), 0)
    parity = (row_id >= rows).astype(jnp.int32)
    degree = own_source * stride + 2 * (v * rows + row_id - parity * rows) + parity
    degrees = degree.astype(F32)
    ratio = degrees * (degrees + 1.0) / (NTRUNC * NTRUNC)
    rate_all = jnp.broadcast_to(rates[...], (8, levels))
    rate_hi, rate_lo = split(rate_all)
    rate_rest = (rate_all - rate_hi.astype(F32) - rate_lo.astype(F32)).astype(BF16)
    rate_row = dot_nn(rate_hi, spread) + dot_nn(rate_lo, spread) + dot_nn(rate_rest, spread)
    damp[...] = 1.0 / (1.0 + rate_row[0:1, :] * ratio)

    def lev_copy(c, k):
        spec, got = ((spec_a, got_a), (spec_b, got_b), (spec_c, got_c))[c]
        return pltpu.make_async_remote_copy(
            src_ref=spec.at[k - 1],
            dst_ref=got.at[v],
            send_sem=lev_send.at[c, k - 1],
            recv_sem=lev_recv.at[c, k - 1],
            device_id={"lev": lax.rem(v + k, lev_count)},
            device_id_type=MESH_IDS,
        )

    def legendre(c):
        first, width, base, length = chunks[c]
        spec, got = ((spec_a, got_a), (spec_b, got_b), (spec_c, got_c))[c]
        for k in wave_steps:
            wave_copy(c, k).wait_recv()

        def store_pair(at, north, southern):
            for p, value in enumerate((north + southern, north - southern)):
                high, low = split(value)
                pair_hi[p, :width, at : at + LANES] = high
                pair_lo[p, :width, at : at + LANES] = low

        half = width // 2
        for q in range(half_waves // 2):
            even = 2 * q
            for e, start in ((even, 0), (even + 1, tiles * LANES + LANES)):
                for t in range(tiles):
                    at = slice(base + t * width, base + (t + 1) * width)
                    store_pair(
                        q * 2 * lats + start + t * LANES,
                        arrived[e, at, :],
                        arrived[wave_count - 1 - e, at, :],
                    )
            ends = slice(base + tiles * width, base + tiles * width + half)

            def middle(one, two):
                a, b = arrived[one, ends, :], arrived[two, ends, :]
                top = jnp.concatenate([a[:, :HALF_TILE], b[:, :HALF_TILE]], axis=1)
                low = jnp.concatenate([a[:, HALF_TILE:], b[:, HALF_TILE:]], axis=1)
                return jnp.concatenate([top, low], axis=0)

            store_pair(
                q * 2 * lats + tiles * LANES,
                middle(even, even + 1),
                middle(wave_count - 1 - even, wave_count - 2 - even),
            )

        for k in lev_steps + (0,):
            target = lax.rem(v + k, lev_count)
            at = pl.ds(pl.multiple_of(target * rows, rows), rows)
            values = []
            for p in range(2):
                l_hi, l_lo = table_hi[p, at, :], table_lo[p, at, :]
                p_hi, p_lo = pair_hi[p, :width, :], pair_lo[p, :width, :]
                values.append(dot_nt(l_hi, p_hi) + dot_nt(l_hi, p_lo) + dot_nt(l_lo, p_hi))
            value = jnp.concatenate(values, axis=1 if width == NARROW else 0)
            if k:
                spec[k - 1] = value
            else:
                got[v] = value
            if k:
                lev_copy(c, k).start()

    def block(c, u):
        value = (got_a, got_b, got_c)[c][u]
        if chunks[c][1] == NARROW:
            value = jnp.concatenate([value[:, :NARROW], value[:, NARROW:]], axis=0)
        return value

    def project(c):
        first, width, base, length = chunks[c]
        for k in lev_steps:
            lev_copy(c, k).wait_recv()
        total = jnp.zeros((2 * rows, mode_cols), F32)
        for u in range(lev_count):
            high, low = split(block(c, u))
            at = slice(u * cols + first, u * cols + first + width)
            total += dot_nn(high, m_hi[at, :]) + dot_nn(high, m_lo[at, :]) + dot_nn(low, m_hi[at, :])
        return total

    legendre(0)
    legendre(1)
    modal[...] = project(0) + project(1)
    legendre(2)
    damped = (modal[...] + project(2)) * damp[...]
    d_hi, d_lo = split(damped)
    pieces = []
    for u in range(lev_count):
        for c in range(len(chunks)):
            pieces.append(block(c, u))
    spectra = jnp.concatenate(pieces, axis=1)
    added = dot_nn(d_hi, g_hi[...]) + dot_nn(d_hi, g_lo[...]) + dot_nn(d_lo, g_hi[...])
    field_row = lax.div(lax.rem(iota((1, all_cols), 1), group), 2)
    result = jnp.where(field_row == 1, 0.0, spectra) + added
    result = jnp.where(degree < NTRUNC, result, 0.0)
    out[0, 0] = result[:rows]
    out[0, 1] = result[rows:]

    for c in range(len(chunks)):
        for k in wave_steps:
            wave_copy(c, k).wait_send()
        for k in lev_steps:
            lev_copy(c, k).wait_send()


def kernel_fits(wave_count, lats, cols, slot_count, half_rows, lat_half, lev_count):
    head = cols - 2 * NARROW
    return (
        slot_count == 1
        and wave_count % 4 == 0
        and lats % LANES == HALF_TILE
        and lats > LANES
        and lat_half == lats * wave_count // 2
        and head > NARROW
        and head % 16 == 0
        and lev_count > 1
        and half_rows % (16 * lev_count) == 0
        and half_rows % 32 == 0
    )


def centre_out(count):
    return tuple(sorted(range(1, count), key=lambda k: (abs(2 * k - count), k)))


def on_device(
    fourier,
    weights,
    row_points,
    slot_map,
    legendre_lookup,
    to_modes,
    from_modes,
    mode_rates,
    thermal_response_matrix,
):
    wave_count = lax.axis_size("wave")
    lev_count = lax.axis_size("lev")
    lats, window, cols = fourier.shape
    slot_count, _, half_rows, lat_half = legendre_lookup.shape
    if not kernel_fits(wave_count, lats, cols, slot_count, half_rows, lat_half, lev_count):
        return on_device_plain(
            fourier,
            weights,
            row_points,
            slot_map,
            legendre_lookup,
            to_modes,
            from_modes,
            mode_rates,
            thermal_response_matrix,
        )
    levels = to_modes.shape[0]
    rows = half_rows // lev_count
    tiles = lats // LANES
    chunks = []
    base = 0
    first = 0
    for width in (cols - 2 * NARROW, NARROW, NARROW):
        length = tiles * width + width // 2
        chunks.append((first, width, base, length))
        first += width
        base += length
    widest = chunks[0][1]
    wide, narrow = (2 * rows, widest), (rows, 2 * NARROW)
    all_cols = cols * lev_count
    mode_cols = 2 * levels
    sizes = (wave_count, lev_count, tuple(chunks), tuple(range(1, wave_count)), centre_out(lev_count))
    vmem = pl.BlockSpec(memory_space=pltpu.VMEM)
    hbm = pl.BlockSpec(memory_space=pl.ANY)
    out_shape = (1, 2, rows, all_cols)
    work = 2 * 3 * 2 * half_rows * lat_half * cols
    return pl.pallas_call(
        functools.partial(kernel, sizes),
        out_shape=jax.ShapeDtypeStruct(out_shape, F32),
        in_specs=[hbm, vmem, vmem] + [hbm] * 6,
        out_specs=vmem,
        scratch_shapes=[
            pltpu.SMEM((window,), jnp.int32),
            *(pltpu.VMEM((window, chunk[1], lats), F32) for chunk in chunks),
            pltpu.VMEM((levels, levels), F32),
            pltpu.VMEM((levels, levels), F32),
            pltpu.VMEM((1, levels), F32),
            pltpu.VMEM((levels, levels), F32),
            pltpu.VMEM((2, half_rows, lat_half), F32),
            pltpu.VMEM((2, half_rows, lat_half), BF16),
            pltpu.VMEM((2, half_rows, lat_half), BF16),
            pltpu.VMEM((wave_count - 1, base, LANES), F32),
            pltpu.VMEM((wave_count, base, LANES), F32),
            pltpu.VMEM((2, widest, lat_half), BF16),
            pltpu.VMEM((2, widest, lat_half), BF16),
            pltpu.VMEM((lev_count - 1, *wide), F32),
            pltpu.VMEM((lev_count - 1, *narrow), F32),
            pltpu.VMEM((lev_count - 1, *narrow), F32),
            pltpu.VMEM((lev_count, *wide), F32),
            pltpu.VMEM((lev_count, *narrow), F32),
            pltpu.VMEM((lev_count, *narrow), F32),
            pltpu.VMEM((all_cols, mode_cols), BF16),
            pltpu.VMEM((all_cols, mode_cols), BF16),
            pltpu.VMEM((mode_cols, all_cols), BF16),
            pltpu.VMEM((mode_cols, all_cols), BF16),
            pltpu.VMEM((2 * rows, mode_cols), F32),
            pltpu.VMEM((2 * rows, mode_cols), F32),
            pltpu.SemaphoreType.DMA((5,)),
            pltpu.SemaphoreType.DMA((len(chunks),)),
            pltpu.SemaphoreType.DMA,
            pltpu.SemaphoreType.DMA((len(chunks), wave_count - 1)),
            pltpu.SemaphoreType.DMA((len(chunks), wave_count - 1)),
            pltpu.SemaphoreType.DMA((len(chunks), lev_count - 1)),
            pltpu.SemaphoreType.DMA((len(chunks), lev_count - 1)),
        ],
        compiler_params=pltpu.CompilerParams(
            collective_id=0, has_side_effects=True, vmem_limit_bytes=56 * 2**20
        ),
        cost_estimate=pl.CostEstimate(flops=work, bytes_accessed=2**24, transcendentals=0),
    )(
        slot_map,
        weights.reshape(1, lats),
        row_points.reshape(wave_count, lats),
        jnp.transpose(fourier, (1, 2, 0)),
        legendre_lookup[0],
        to_modes,
        from_modes,
        mode_rates.reshape(1, levels),
        thermal_response_matrix,
    )


def solution(mesh):
    placed = (
        P("wave", None, "lev"),
        P("wave"),
        P(),
        P(),
        P("wave", None, None, None),
        P(),
        P(),
        P(),
        P(),
    )
    return jax.shard_map(
        on_device,
        mesh=mesh,
        in_specs=placed,
        out_specs=P("wave", None, "lev", None),
        check_vma=False,
    )
```

```python
import functools
import jax
import jax.numpy as jnp
from jax import lax
from jax.experimental import pallas as pl
from jax.experimental.pallas import tpu as pltpu
from jax.sharding import PartitionSpec as P

NTRUNC = 1280
LEVELS = 136
FIELDS = 4


def vertical_step(spectra, degree, to_modes, from_modes, mode_rates, thermal_response_matrix):
    maximal_wave_truncation = lax.Precision.HIGHEST
    layerwise_coefficients = spectra.reshape(spectra.shape[:-1] + (LEVELS, FIELDS, 2))
    divergence = layerwise_coefficients[..., 1, :]
    modal = jnp.einsum("kl,...lc->...kc", to_modes, divergence, precision=maximal_wave_truncation)
    degrees = degree.astype(jnp.float32)
    wave_ratio = degrees * (degrees + 1.0) / (NTRUNC * NTRUNC)
    damping = 1.0 / (1.0 + mode_rates * wave_ratio[..., None])
    advanced_flow_spreading = jnp.einsum(
        "mc,...cb->...mb", from_modes, modal * damping[..., None], precision=maximal_wave_truncation
    )
    advanced_thermal_field = layerwise_coefficients[..., 2, :] - jnp.einsum(
        "mc,...cb->...mb",
        thermal_response_matrix,
        advanced_flow_spreading,
        precision=maximal_wave_truncation,
    )
    joined_coefficient_sets = jnp.stack(
        [
            layerwise_coefficients[..., 0, :],
            advanced_flow_spreading,
            advanced_thermal_field,
            layerwise_coefficients[..., 3, :],
        ],
        axis=-2,
    )
    return joined_coefficient_sets.reshape(spectra.shape)


def legendre_sums(paired, tables):
    maximal_wave_truncation = lax.Precision.HIGHEST
    return jnp.einsum("spih,phsc->spic", tables, paired, precision=maximal_wave_truncation)


def on_device_plain(
    fourier,
    weights,
    row_points,
    slot_map,
    legendre_lookup,
    to_modes,
    from_modes,
    mode_rates,
    thermal_response_matrix,
):
    wave_count = lax.axis_size("wave")
    layer_number = lax.axis_size("lev")
    wave_index = lax.axis_index("wave")
    level_index = lax.axis_index("lev")
    lat_local = fourier.shape[0]
    window = fourier.shape[1]
    columns = fourier.shape[2]
    slot_count = legendre_lookup.shape[0]
    half_rows = legendre_lookup.shape[2]
    lat_half = legendre_lookup.shape[3]
    all_slots = slot_count * wave_count
    lat_total = 2 * lat_half
    stride = NTRUNC // window
    wavenum = jnp.arange(window, dtype=jnp.int32) * stride
    points_here = lax.dynamic_slice_in_dim(row_points, wave_index * lat_local, lat_local, 0)
    retained = (2 * wavenum[None, :] < points_here[:, None]).astype(jnp.float32)
    weighted = fourier * (weights[:, None] * retained)[:, :, None]
    slot_ids = jnp.arange(all_slots, dtype=jnp.int32)
    matches = (slot_map[None, :] == slot_ids[:, None]).astype(jnp.int32)
    used_all = jnp.sum(matches, axis=1)
    source_all = jnp.sum(matches * jnp.arange(window, dtype=jnp.int32)[None, :], axis=1)
    outgoing = jnp.take(weighted, source_all, axis=1) * used_all.astype(jnp.float32)[None, :, None]
    outgoing = outgoing.reshape(lat_local, wave_count, slot_count, columns)
    arrived = lax.all_to_all(outgoing, "wave", split_axis=1, concat_axis=0, tiled=True)
    arrived = arrived.reshape(lat_total, slot_count, columns)
    northern = arrived[:lat_half]
    southern = arrived[lat_half:][::-1]
    paired = jnp.stack([northern + southern, northern - southern])
    owned_orders = lax.dynamic_slice_in_dim(source_all, wave_index * slot_count, slot_count, 0)
    degree_base = owned_orders * stride
    row_count = half_rows // layer_number
    row_start = level_index * row_count
    local_spectra = legendre_sums(paired, legendre_lookup)
    spectra = lax.all_to_all(local_spectra, "lev", split_axis=2, concat_axis=3, tiled=True)
    row_ids = row_start + jnp.arange(row_count, dtype=jnp.int32)
    parities = jnp.arange(2, dtype=jnp.int32)
    degree = degree_base[:, None, None] + 2 * row_ids[None, None, :] + parities[None, :, None]
    validity = (degree < NTRUNC).astype(jnp.float32)
    joined_coefficient_sets = vertical_step(
        spectra, degree, to_modes, from_modes, mode_rates, thermal_response_matrix
    )
    return joined_coefficient_sets * validity[..., None]


F32 = jnp.float32
BF16 = jnp.bfloat16
HALF_TILE = 64
LANES = 128
NARROW = 64
MESH_IDS = pl.DeviceIdType.MESH


def split(x):
    high = x.astype(BF16)
    return high, (x - high.astype(F32)).astype(BF16)


def dot_nn(a, b):
    return lax.dot_general(a, b, (((1,), (0,)), ((), ())), preferred_element_type=F32)


def dot_nt(a, b):
    return lax.dot_general(a, b, (((1,), (1,)), ((), ())), preferred_element_type=F32)


def iota(shape, dim):
    return lax.broadcasted_iota(jnp.int32, shape, dim)


def one_hot(cond):
    return cond.astype(F32).astype(BF16)


def kernel(
    sizes,
    slot_hbm,
    weights,
    points,
    fourier_hbm,
    table_hbm,
    to_hbm,
    from_hbm,
    rates_hbm,
    thermal_hbm,
    out,
    slot_map,
    fourier_a,
    fourier_b,
    fourier_c,
    to_modes,
    from_modes,
    rates,
    thermal,
    table,
    table_hi,
    table_lo,
    outgoing,
    arrived,
    pair_hi,
    pair_lo,
    spec_a,
    spec_b,
    spec_c,
    got_a,
    got_b,
    got_c,
    m_hi,
    m_lo,
    g_hi,
    g_lo,
    damp,
    modal,
    small_sem,
    fourier_sem,
    table_sem,
    wave_send,
    wave_recv,
    lev_send,
    lev_recv,
):
    wave_count, lev_count, chunks, wave_steps, lev_steps = sizes
    window, cols, lats = fourier_hbm.shape
    fouriers = (fourier_a, fourier_b, fourier_c)
    _, half_rows, lat_half = table_hbm.shape
    levels = to_modes.shape[0]
    all_cols = cols * lev_count
    mode_cols = 2 * levels
    rows = half_rows // lev_count
    stride = NTRUNC // window
    tiles = lats // LANES
    half_waves = wave_count // 2
    w = lax.axis_index("wave")
    v = lax.axis_index("lev")

    barrier = pltpu.get_barrier_semaphore()
    for k in wave_steps:
        pl.semaphore_signal(
            barrier, inc=1, device_id={"wave": lax.rem(w + k, wave_count)}, device_id_type=MESH_IDS
        )
    for k in lev_steps:
        pl.semaphore_signal(
            barrier, inc=1, device_id={"lev": lax.rem(v + k, lev_count)}, device_id_type=MESH_IDS
        )
    slot_copy = pltpu.make_async_copy(slot_hbm, slot_map, small_sem.at[0])
    slot_copy.start()
    fourier_copies = []
    for c, (first, width, base, length) in enumerate(chunks):
        at = slice(first, first + width)
        fourier_copies.append(
            pltpu.make_async_copy(fourier_hbm.at[:, at], fouriers[c], fourier_sem.at[c])
        )
        fourier_copies[c].start()
    small_copies = []
    for n, (there, here) in enumerate(
        ((to_hbm, to_modes), (from_hbm, from_modes), (rates_hbm, rates), (thermal_hbm, thermal))
    ):
        small_copies.append(pltpu.make_async_copy(there, here, small_sem.at[n + 1]))
        small_copies[n].start()
    table_copy = pltpu.make_async_copy(table_hbm, table, table_sem)
    table_copy.start()

    def slot_source(slot):
        source = jnp.int32(0)
        used = jnp.int32(0)
        for j in range(window):
            hit = slot_map[j] == slot
            source = jnp.where(hit, j, source)
            used = jnp.where(hit, 1, used)
        return source, used

    south = (w >= half_waves).astype(jnp.int32)
    mirrored = w + south * (wave_count - 1 - 2 * w)
    odd = lax.rem(mirrored, 2)
    place = iota((lats, lats), 1) + odd * HALF_TILE
    place = jnp.where(place >= lats, place - lats, place)
    place = place + south * (lats - 1 - 2 * place)
    arrange = one_hot(iota((lats, lats), 0) == place)
    point_row = points[pl.ds(w, 1), :]
    weight_row = weights[...]
    slot_copy.wait()

    def arranged(slot, c, width, write):
        source, used = slot_source(slot)
        keep = (2 * stride * source < point_row).astype(F32) * used.astype(F32)
        block = fouriers[c][source] * (weight_row * keep)
        high, low = split(block)
        moved = dot_nn(high, arrange) + dot_nn(low, arrange)
        for t in range(tiles):
            write(t * width, width, moved[:, t * LANES : (t + 1) * LANES])
        left = moved[: width // 2, tiles * LANES :]
        right = moved[width // 2 :, tiles * LANES :]
        write(tiles * width, width // 2, jnp.concatenate([left, right], axis=1))

    def wave_copy(c, k):
        first, width, base, length = chunks[c]
        return pltpu.make_async_remote_copy(
            src_ref=outgoing.at[k - 1, pl.ds(base, length)],
            dst_ref=arrived.at[w, pl.ds(base, length)],
            send_sem=wave_send.at[c, k - 1],
            recv_sem=wave_recv.at[c, k - 1],
            device_id={"wave": lax.rem(w + k, wave_count)},
            device_id_type=MESH_IDS,
        )

    for c, (first, width, base, length) in enumerate(chunks):
        fourier_copies[c].wait()
        for k in wave_steps:

            def put(at, count, value, k=k, base=base):
                outgoing[k - 1, base + at : base + at + count, :] = value

            arranged(lax.rem(w + k, wave_count), c, width, put)
            if c == 0 and k == wave_steps[0]:
                pl.semaphore_wait(barrier, len(wave_steps) + len(lev_steps))
            wave_copy(c, k).start()
    for c, (first, width, base, length) in enumerate(chunks):

        def put_own(at, count, value, base=base):
            arrived[w, base + at : base + at + count, :] = value

        arranged(w, c, width, put_own)

    table_copy.wait()
    step_rows = 32

    @pl.loop(0, half_rows // step_rows)
    def _(r):
        at = pl.ds(pl.multiple_of(r * step_rows, step_rows), step_rows)
        for p in range(2):
            high, low = split(table[p, at, :])
            table_hi[p, at, :] = high
            table_lo[p, at, :] = low

    for copy in small_copies:
        copy.wait()
    part_mask = (
        lax.rem(iota((all_cols, mode_cols), 0), 2) == lax.rem(iota((all_cols, mode_cols), 1), 2)
    ).astype(F32)
    part_mask_t = (
        lax.rem(iota((mode_cols, all_cols), 0), 2) == lax.rem(iota((mode_cols, all_cols), 1), 2)
    ).astype(F32)
    group = 2 * FIELDS
    col_id = iota((all_cols, levels), 0)
    take_level = one_hot(
        (lax.div(col_id, group) == iota((all_cols, levels), 1))
        & (lax.div(lax.rem(col_id, group), 2) == 1)
    )
    spread = one_hot(lax.div(iota((levels, mode_cols), 1), 2) == iota((levels, mode_cols), 0))
    for piece, held in zip(split(to_modes[...]), (m_hi, m_lo)):
        picked = dot_nt(take_level, piece).astype(BF16)
        held[...] = (dot_nn(picked, spread) * part_mask).astype(BF16)

    from_hi, from_lo = split(from_modes[...])
    th_hi, th_lo = split(thermal[...])
    response = -(dot_nn(th_hi, from_hi) + dot_nn(th_hi, from_lo) + dot_nn(th_lo, from_hi))
    resp_hi, resp_lo = split(response)
    spread_t = one_hot(lax.div(iota((mode_cols, levels), 0), 2) == iota((mode_cols, levels), 1))
    lane_id = iota((levels, all_cols), 1)
    same_level = lax.div(lane_id, group) == iota((levels, all_cols), 0)
    field = lax.div(lax.rem(lane_id, group), 2)
    put_div = one_hot(same_level & (field == 1))
    put_temp = one_hot(same_level & (field == 2))
    for div_piece, temp_piece, held in ((from_hi, resp_hi, g_hi), (from_lo, resp_lo, g_lo)):
        div_cols = dot_nt(spread_t, div_piece).astype(BF16)
        temp_cols = dot_nt(spread_t, temp_piece).astype(BF16)
        both = dot_nn(div_cols, put_div) + dot_nn(temp_cols, put_temp)
        held[...] = (both * part_mask_t).astype(BF16)

    own_source, _ = slot_source(w)
    row_id = iota((2 * rows, 1), 0)
    parity = (row_id >= rows).astype(jnp.int32)
    degree = own_source * stride + 2 * (v * rows + row_id - parity * rows) + parity
    degrees = degree.astype(F32)
    ratio = degrees * (degrees + 1.0) / (NTRUNC * NTRUNC)
    rate_all = jnp.broadcast_to(rates[...], (8, levels))
    rate_hi, rate_lo = split(rate_all)
    rate_rest = (rate_all - rate_hi.astype(F32) - rate_lo.astype(F32)).astype(BF16)
    rate_row = dot_nn(rate_hi, spread) + dot_nn(rate_lo, spread) + dot_nn(rate_rest, spread)
    damp[...] = 1.0 / (1.0 + rate_row[0:1, :] * ratio)

    def lev_copy(c, k):
        spec, got = ((spec_a, got_a), (spec_b, got_b), (spec_c, got_c))[c]
        return pltpu.make_async_remote_copy(
            src_ref=spec.at[k - 1],
            dst_ref=got.at[v],
            send_sem=lev_send.at[c, k - 1],
            recv_sem=lev_recv.at[c, k - 1],
            device_id={"lev": lax.rem(v + k, lev_count)},
            device_id_type=MESH_IDS,
        )

    def legendre(c):
        first, width, base, length = chunks[c]
        spec, got = ((spec_a, got_a), (spec_b, got_b), (spec_c, got_c))[c]
        for k in wave_steps:
            wave_copy(c, k).wait_recv()

        def store_pair(at, north, southern):
            for p, value in enumerate((north + southern, north - southern)):
                high, low = split(value)
                pair_hi[p, :width, at : at + LANES] = high
                pair_lo[p, :width, at : at + LANES] = low

        half = width // 2
        for q in range(half_waves // 2):
            even = 2 * q
            for e, start in ((even, 0), (even + 1, tiles * LANES + LANES)):
                for t in range(tiles):
                    at = slice(base + t * width, base + (t + 1) * width)
                    store_pair(
                        q * 2 * lats + start + t * LANES,
                        arrived[e, at, :],
                        arrived[wave_count - 1 - e, at, :],
                    )
            ends = slice(base + tiles * width, base + tiles * width + half)

            def middle(one, two):
                a, b = arrived[one, ends, :], arrived[two, ends, :]
                top = jnp.concatenate([a[:, :HALF_TILE], b[:, :HALF_TILE]], axis=1)
                low = jnp.concatenate([a[:, HALF_TILE:], b[:, HALF_TILE:]], axis=1)
                return jnp.concatenate([top, low], axis=0)

            store_pair(
                q * 2 * lats + tiles * LANES,
                middle(even, even + 1),
                middle(wave_count - 1 - even, wave_count - 2 - even),
            )

        for k in lev_steps + (0,):
            target = lax.rem(v + k, lev_count)
            at = pl.ds(pl.multiple_of(target * rows, rows), rows)
            values = []
            for p in range(2):
                l_hi, l_lo = table_hi[p, at, :], table_lo[p, at, :]
                p_hi, p_lo = pair_hi[p, :width, :], pair_lo[p, :width, :]
                values.append(dot_nt(l_hi, p_hi) + dot_nt(l_hi, p_lo) + dot_nt(l_lo, p_hi))
            value = jnp.concatenate(values, axis=1 if width == NARROW else 0)
            if k:
                spec[k - 1] = value
            else:
                got[v] = value
            if k:
                lev_copy(c, k).start()

    def block(c, u):
        value = (got_a, got_b, got_c)[c][u]
        if chunks[c][1] == NARROW:
            value = jnp.concatenate([value[:, :NARROW], value[:, NARROW:]], axis=0)
        return value

    def project(c):
        first, width, base, length = chunks[c]
        for k in lev_steps:
            lev_copy(c, k).wait_recv()
        total = jnp.zeros((2 * rows, mode_cols), F32)
        for u in range(lev_count):
            high, low = split(block(c, u))
            at = slice(u * cols + first, u * cols + first + width)
            total += dot_nn(high, m_hi[at, :]) + dot_nn(high, m_lo[at, :]) + dot_nn(low, m_hi[at, :])
        return total

    legendre(0)
    legendre(1)
    modal[...] = project(0) + project(1)
    legendre(2)
    damped = (modal[...] + project(2)) * damp[...]
    d_hi, d_lo = split(damped)
    pieces = []
    for u in range(lev_count):
        for c in range(len(chunks)):
            pieces.append(block(c, u))
    spectra = jnp.concatenate(pieces, axis=1)
    added = dot_nn(d_hi, g_hi[...]) + dot_nn(d_hi, g_lo[...]) + dot_nn(d_lo, g_hi[...])
    field_row = lax.div(lax.rem(iota((1, all_cols), 1), group), 2)
    result = jnp.where(field_row == 1, 0.0, spectra) + added
    result = jnp.where(degree < NTRUNC, result, 0.0)
    out[0, 0] = result[:rows]
    out[0, 1] = result[rows:]

    for c in range(len(chunks)):
        for k in wave_steps:
            wave_copy(c, k).wait_send()
        for k in lev_steps:
            lev_copy(c, k).wait_send()


def kernel_fits(wave_count, lats, cols, slot_count, half_rows, lat_half, lev_count):
    head = cols - 2 * NARROW
    return (
        slot_count == 1
        and wave_count % 4 == 0
        and lats % LANES == HALF_TILE
        and lats > LANES
        and lat_half == lats * wave_count // 2
        and head > NARROW
        and head % 16 == 0
        and lev_count > 1
        and half_rows % (16 * lev_count) == 0
        and half_rows % 32 == 0
    )


def centre_out(count):
    return tuple(sorted(range(1, count), key=lambda k: (-abs(2 * k - count), k)))


def on_device(
    fourier,
    weights,
    row_points,
    slot_map,
    legendre_lookup,
    to_modes,
    from_modes,
    mode_rates,
    thermal_response_matrix,
):
    wave_count = lax.axis_size("wave")
    lev_count = lax.axis_size("lev")
    lats, window, cols = fourier.shape
    slot_count, _, half_rows, lat_half = legendre_lookup.shape
    if not kernel_fits(wave_count, lats, cols, slot_count, half_rows, lat_half, lev_count):
        return on_device_plain(
            fourier,
            weights,
            row_points,
            slot_map,
            legendre_lookup,
            to_modes,
            from_modes,
            mode_rates,
            thermal_response_matrix,
        )
    levels = to_modes.shape[0]
    rows = half_rows // lev_count
    tiles = lats // LANES
    chunks = []
    base = 0
    first = 0
    for width in (cols - 2 * NARROW, NARROW, NARROW):
        length = tiles * width + width // 2
        chunks.append((first, width, base, length))
        first += width
        base += length
    widest = chunks[0][1]
    wide, narrow = (2 * rows, widest), (rows, 2 * NARROW)
    all_cols = cols * lev_count
    mode_cols = 2 * levels
    sizes = (wave_count, lev_count, tuple(chunks), centre_out(wave_count), centre_out(lev_count))
    vmem = pl.BlockSpec(memory_space=pltpu.VMEM)
    hbm = pl.BlockSpec(memory_space=pl.ANY)
    out_shape = (1, 2, rows, all_cols)
    work = 2 * 3 * 2 * half_rows * lat_half * cols
    return pl.pallas_call(
        functools.partial(kernel, sizes),
        out_shape=jax.ShapeDtypeStruct(out_shape, F32),
        in_specs=[hbm, vmem, vmem] + [hbm] * 6,
        out_specs=vmem,
        scratch_shapes=[
            pltpu.SMEM((window,), jnp.int32),
            *(pltpu.VMEM((window, chunk[1], lats), F32) for chunk in chunks),
            pltpu.VMEM((levels, levels), F32),
            pltpu.VMEM((levels, levels), F32),
            pltpu.VMEM((1, levels), F32),
            pltpu.VMEM((levels, levels), F32),
            pltpu.VMEM((2, half_rows, lat_half), F32),
            pltpu.VMEM((2, half_rows, lat_half), BF16),
            pltpu.VMEM((2, half_rows, lat_half), BF16),
            pltpu.VMEM((wave_count - 1, base, LANES), F32),
            pltpu.VMEM((wave_count, base, LANES), F32),
            pltpu.VMEM((2, widest, lat_half), BF16),
            pltpu.VMEM((2, widest, lat_half), BF16),
            pltpu.VMEM((lev_count - 1, *wide), F32),
            pltpu.VMEM((lev_count - 1, *narrow), F32),
            pltpu.VMEM((lev_count - 1, *narrow), F32),
            pltpu.VMEM((lev_count, *wide), F32),
            pltpu.VMEM((lev_count, *narrow), F32),
            pltpu.VMEM((lev_count, *narrow), F32),
            pltpu.VMEM((all_cols, mode_cols), BF16),
            pltpu.VMEM((all_cols, mode_cols), BF16),
            pltpu.VMEM((mode_cols, all_cols), BF16),
            pltpu.VMEM((mode_cols, all_cols), BF16),
            pltpu.VMEM((2 * rows, mode_cols), F32),
            pltpu.VMEM((2 * rows, mode_cols), F32),
            pltpu.SemaphoreType.DMA((5,)),
            pltpu.SemaphoreType.DMA((len(chunks),)),
            pltpu.SemaphoreType.DMA,
            pltpu.SemaphoreType.DMA((len(chunks), wave_count - 1)),
            pltpu.SemaphoreType.DMA((len(chunks), wave_count - 1)),
            pltpu.SemaphoreType.DMA((len(chunks), lev_count - 1)),
            pltpu.SemaphoreType.DMA((len(chunks), lev_count - 1)),
        ],
        compiler_params=pltpu.CompilerParams(
            collective_id=0, has_side_effects=True, vmem_limit_bytes=56 * 2**20
        ),
        cost_estimate=pl.CostEstimate(flops=work, bytes_accessed=2**24, transcendentals=0),
    )(
        slot_map,
        weights.reshape(1, lats),
        row_points.reshape(wave_count, lats),
        jnp.transpose(fourier, (1, 2, 0)),
        legendre_lookup[0],
        to_modes,
        from_modes,
        mode_rates.reshape(1, levels),
        thermal_response_matrix,
    )


def solution(mesh):
    placed = (
        P("wave", None, "lev"),
        P("wave"),
        P(),
        P(),
        P("wave", None, None, None),
        P(),
        P(),
        P(),
        P(),
    )
    return jax.shard_map(
        on_device,
        mesh=mesh,
        in_specs=placed,
        out_specs=P("wave", None, "lev", None),
        check_vma=False,
    )
```
